32 devices in a mesh: layer: 4 (over y, core), tx: 2 (over x), ty: 4 (over z).
Axes of the slice: x: 2, y: 2, z: 4, core: 2. Of those that a mesh axis runs over, the one named last changes fastest.
Arguments:
- layers: float32 [4, 256, 2048], P('layer', 'tx', 'ty'), may hold values from -6 to 6
- wind: int32 [4, 2], P('layer'), may hold values from -128 to 128
- offsets: int32 [4, 9, 2], P('layer'), may hold values from -64 to 64
- weights: bfloat16 [9, 2, 256, 2048], P(None, None, 'tx', 'ty'), may hold values from -0.5 to 0.5
- sub_index: int32 [256, 2048], P('tx', 'ty'), may hold values from -1 to 255, as said below
Outputs:
- slopes: float32 [2, 9, 32, 256], P(None, None, 'tx', 'ty')
The draws below stay inside these ranges and needn't reach their ends.
Inputs may be any that keep to these rules, and one draw needn't show every extreme that they name: sub_index[i, j] is -1 or j // 8.
All inputs are finite; a program needn't handle non-finite values.
Results may differ from the reference program's by a relative error of at most 0.0003.
Values sent between devices are 32-bit elements; how exact they have to be, the bound alone decides.
A program may use at most 256 MiB of HBM per device.

```python
import jax
import jax.numpy as jnp
from jax import lax

DIRS = 9
SUB = 8
HMAX = 2
FOOT = 64
LAYERS = 4
NX = 256
NY = 2048


def draw_wind(key, part):
    key_a, key_b, key_c = jax.random.split(jax.random.fold_in(key, 11), 3)
    top = 64 * HMAX
    base = jax.random.randint(key_a, (LAYERS, 2), -top, top + 1)
    high = jax.random.randint(key_b, (1, 2), 0, LAYERS)
    low = (high + 1 + jax.random.randint(key_c, (1, 2), 0, LAYERS - 1)) % LAYERS
    rows = jnp.arange(LAYERS)[:, None]
    base = jnp.where(rows == high, top, base)
    base = jnp.where(rows == low, -top, base)
    return base.astype(jnp.int32)


def draw_offsets(key, part):
    key_a, key_b, key_c = jax.random.split(jax.random.fold_in(key, 23), 3)
    base = jax.random.randint(key_a, (LAYERS, DIRS, 2), -FOOT, FOOT + 1)
    high = jax.random.randint(key_b, (LAYERS, 1, 2), 0, DIRS)
    low = (high + 1 + jax.random.randint(key_c, (LAYERS, 1, 2), 0, DIRS - 1)) % DIRS
    dirs = jnp.arange(DIRS)[None, :, None]
    base = jnp.where(dirs == high, FOOT, base)
    base = jnp.where(dirs == low, -FOOT, base)
    return base.astype(jnp.int32)


def draw_sub_index(key, part):
    rows = jnp.arange(NX)[:, None]
    cols = jnp.arange(NY)[None, :]
    column = jnp.broadcast_to(cols // SUB, (NX, NY))
    dead = jax.random.randint(jax.random.fold_in(key, 37), (NX, NY), 0, 8) == 0
    corner_first = (rows == 0) & (cols == 0)
    corner_last = (rows == NX - 1) & (cols == NY - 1)
    dead = (dead | corner_first) & jnp.logical_not(corner_last)
    return jnp.where(dead, -1, column).astype(jnp.int32)


def shard_levels(own_key, shape, cuts, least, largest):
    def one(axis_at, shards_of):
        draws = jax.random.uniform(jax.random.fold_in(jax.random.fold_in(own_key, 6), axis_at), (shards_of,), jnp.float32, least / len(cuts), largest / len(cuts))
        return jnp.repeat(jnp.exp(draws), shape[axis_at] // shards_of).reshape((-1,) + (1,) * (len(shape) - axis_at - 1))

    gain = one(*cuts[0])
    for cut in cuts[1:]:
        gain = gain * one(*cut)
    return gain


def scatter_about(stream_key, dims, scale, limit, cuts=(), dtype=jnp.bfloat16):
    array = jax.random.normal(stream_key, dims, jnp.float32) * scale
    if len(cuts) > 0:
        array = shard_levels(stream_key, dims, cuts, -0.22, 0.18) * array
    return jnp.clip(array, min=-limit, max=limit).astype(dtype)


def setup_inputs(seed: int = 0) -> dict:
    key_of = jax.random.split(jax.random.key(seed), 6)
    layers = scatter_about(key_of[0], (LAYERS, NX, NY), 1.0, 6.0, ((0, 4), (1, 2), (2, 4)), jnp.float32)
    wind = draw_wind(jax.random.fold_in(key_of[5], 71), 0)
    offsets = draw_offsets(jax.random.fold_in(key_of[5], 71), 0)
    weights = scatter_about(key_of[3], (DIRS, 2, NX, NY), 0.03125, 0.5, ((2, 2), (3, 4)))
    sub_index = draw_sub_index(jax.random.fold_in(key_of[5], 71), 0)
    return dict(layers=layers, wind=wind, offsets=offsets, weights=weights, sub_index=sub_index)


def reference(layers, wind, offsets, weights, sub_index):
    quotient = jnp.floor_divide(wind, 64).astype(jnp.int32)
    fraction = (wind - 64 * quotient).astype(jnp.float32) / 64.0
    live = (sub_index >= 0).astype(jnp.float32)

    def one_layer(total, item):
        field, whole, part, moves = item
        qrow = whole[0]
        qcol = whole[1]
        frow = part[0]
        fcol = part[1]
        corner_aa = jnp.roll(field, (qrow, qcol), (0, 1))
        corner_ab = jnp.roll(field, (qrow, qcol + 1), (0, 1))
        corner_ba = jnp.roll(field, (qrow + 1, qcol), (0, 1))
        corner_bb = jnp.roll(field, (qrow + 1, qcol + 1), (0, 1))
        shifted = (1.0 - frow) * ((1.0 - fcol) * corner_aa + fcol * corner_ab) + frow * ((1.0 - fcol) * corner_ba + fcol * corner_bb)
        views = jnp.stack([jnp.roll(shifted, (-moves[d, 0], -moves[d, 1]), (0, 1)) for d in range(DIRS)])
        return total + views, None

    start = jnp.zeros((DIRS, NX, NY), jnp.float32)
    total, _ = lax.scan(one_layer, start, (layers, quotient, fraction, offsets))
    masked = total * live
    terms = weights.astype(jnp.float32) * masked[:, None]
    sums = terms.reshape(DIRS, 2, NX // SUB, SUB, NY // SUB, SUB).sum(axis=(3, 5))
    return jnp.transpose(sums, (1, 0, 2, 3))
```

```python
import functools

import jax
import jax.numpy as jnp
from jax import lax
from jax.experimental import pallas as pl
from jax.experimental.pallas import tpu as pltpu
from jax.sharding import PartitionSpec as P

DIRS = 9
SUB = 8
HMAX = 2
FOOT = 64
LANES = 128
RIM = 72
MESH = pl.DeviceIdType.MESH


def kernel(
    sizes, wind, offsets, layers, weights, sub_index, out, field, shifted, wraw, wlive, sub, parts,
    local_sem, xs_sem, xr_sem, zs_sem, zr_sem, ss_sem, sr_sem,
):
    n_layer, n_tx, n_ty = sizes
    rows, cols = sub_index.shape
    tiles = cols // LANES
    groups = rows // SUB
    last = tiles + 1
    foot_rows = RIM if n_tx > 2 else rows - RIM
    layer = lax.axis_index("layer")
    tx = lax.axis_index("tx")
    ty = lax.axis_index("ty")
    up = {"tx": lax.rem(tx + n_tx - 1, n_tx)}
    down = {"tx": lax.rem(tx + 1, n_tx)}
    left = {"ty": lax.rem(ty + n_ty - 1, n_ty)}
    right = {"ty": lax.rem(ty + 1, n_ty)}
    peers = [{"layer": lax.rem(layer + k, n_layer)} for k in range(1, n_layer)]

    own = []
    for c in range(tiles):
        copy = pltpu.make_async_copy(
            layers.at[0, :, pl.ds(c * LANES, LANES)],
            field.at[c + 1, pl.ds(RIM, rows), :],
            local_sem.at[c],
        )
        copy.start()
        own.append(copy)
    sub_copy = pltpu.make_async_copy(sub_index, sub, local_sem.at[tiles])
    sub_copy.start()
    weight_copy = pltpu.make_async_copy(weights, wraw, local_sem.at[tiles + 1])
    weight_copy.start()

    barrier = pltpu.get_barrier_semaphore()
    greeted = [up, left, right] if n_tx == 2 else [up, down, left, right]
    for device in greeted + peers:
        pl.semaphore_signal(barrier, inc=1, device_id=device, device_id_type=MESH)
    pl.semaphore_wait(barrier, len(greeted) + len(peers))

    def send(src, dst, send_sem, recv_sem, device):
        copy = pltpu.make_async_remote_copy(
            src_ref=src, dst_ref=dst, send_sem=send_sem, recv_sem=recv_sem,
            device_id=device, device_id_type=MESH,
        )
        copy.start()
        return copy

    def send_rows(c):
        return [
            send(
                field.at[c, pl.ds(rows, RIM), :], field.at[c, pl.ds(0, RIM), :],
                xs_sem.at[c - 1, 0], xr_sem.at[c - 1, 0], down,
            ),
            send(
                field.at[c, pl.ds(RIM, foot_rows), :], field.at[c, pl.ds(RIM + rows, foot_rows), :],
                xs_sem.at[c - 1, 1], xr_sem.at[c - 1, 1], up,
            ),
        ]

    def send_cols(start, size, k):
        return [
            send(
                field.at[tiles, pl.ds(start, size), :], field.at[0, pl.ds(start, size), :],
                zs_sem.at[0, k], zr_sem.at[0, k], right,
            ),
            send(
                field.at[1, pl.ds(start, size), :], field.at[last, pl.ds(start, size), :],
                zs_sem.at[1, k], zr_sem.at[1, k], left,
            ),
        ]

    for copy in own:
        copy.wait()
    edge_copies = send_rows(1) + send_rows(tiles)
    col_copies = send_cols(RIM, rows, 0)
    mid_copies = []
    for c in range(2, tiles):
        mid_copies += send_rows(c)

    sub_copy.wait()
    weight_copy.wait()

    def prepare(d, carry):
        for c in range(tiles):
            for g in range(0, groups, 2):
                live = (sub[pl.ds(g * SUB, 2 * SUB), pl.ds(c * LANES, LANES)] >= 0).astype(jnp.float32)
                for s in range(2):
                    both = wraw[d, s, pl.ds(g * SUB, 2 * SUB), pl.ds(c * LANES, LANES)].astype(jnp.float32) * live
                    for h in range(2):
                        wlive[d, s, c, pl.ds(g + h, SUB, stride=groups), :] = both[h * SUB : (h + 1) * SUB]
        return carry

    lax.fori_loop(0, 4, prepare, 0)
    for copy in edge_copies:
        copy.wait_recv()
    col_copies += send_cols(0, RIM, 1) + send_cols(RIM + rows, foot_rows, 2)
    lax.fori_loop(4, DIRS, prepare, 0)

    for copy in mid_copies:
        copy.wait_recv()
    for copy in col_copies:
        copy.wait_recv()
    if n_tx == 2:
        for c in range(tiles + 2):
            field[c, pl.ds(RIM + rows + foot_rows, RIM - foot_rows), :] = field[c, pl.ds(0, RIM - foot_rows), :]

    wide = rows // SUB + 2 * FOOT // SUB
    qrow = lax.shift_right_arithmetic(wind[0, 0], 6)
    qcol = lax.shift_right_arithmetic(wind[0, 1], 6)
    frow = (wind[0, 0] - 64 * qrow).astype(jnp.float32) / 64.0
    fcol = (wind[0, 1] - 64 * qcol).astype(jnp.float32) / 64.0
    lead = HMAX + 1 - qcol
    lane = lax.broadcasted_iota(jnp.int32, (wide, LANES), 1)

    def shift_phase(p, carry):
        mixed = []
        for c in range(tiles + 2):
            here = field[c, pl.ds(RIM - FOOT + p - qrow, wide, stride=SUB), :]
            above = field[c, pl.ds(RIM - FOOT - 1 + p - qrow, wide, stride=SUB), :]
            mixed.append((1.0 - frow) * here + frow * above)
        first = [pltpu.roll(m, (LANES - lead) & (LANES - 1), 1) for m in mixed]
        second = [pltpu.roll(m, (LANES + 1 - lead) & (LANES - 1), 1) for m in mixed]
        for c in range(tiles + 2):
            after = min(c + 1, last)
            one = jnp.where(lane < LANES - lead, first[c], first[after])
            two = jnp.where(lane < LANES + 1 - lead, second[c], second[after])
            shifted[c, p, :, :] = (1.0 - fcol) * one + fcol * two
        return carry

    lax.fori_loop(0, SUB, shift_phase, 0)

    lane_g = lax.broadcasted_iota(jnp.int32, (groups, LANES), 1)
    half = cols // SUB
    pick_row = lax.broadcasted_iota(jnp.int32, (cols, LANES), 0)
    pick_col = lax.broadcasted_iota(jnp.int32, (cols, LANES), 1)
    pick = (lax.shift_right_logical(pick_row, 3) == (pick_col & (half - 1))).astype(jnp.bfloat16)

    def slopes(d, carry):
        top = offsets[0, d, 0] + FOOT
        begin = offsets[0, d, 1] + LANES - HMAX - 1
        base = lax.shift_right_arithmetic(begin, 7)
        skip = begin & (LANES - 1)
        turn = (LANES - skip) & (LANES - 1)
        sums = [[None] * tiles for _ in range(2)]
        for r in range(SUB):
            row = top + r
            phase = row & (SUB - 1)
            first = lax.shift_right_arithmetic(row, 3)
            turned = [
                pltpu.roll(shifted[base + c, phase, pl.ds(first, groups), :], turn, 1) for c in range(tiles + 1)
            ]
            for c in range(tiles):
                view = jnp.where(lane_g < LANES - skip, turned[c], turned[c + 1])
                for s in range(2):
                    term = wlive[d, s, c, pl.ds(r * groups, groups), :] * view
                    sums[s][c] = term if r == 0 else sums[s][c] + term
        rows_of = []
        for s in range(2):
            total = jnp.concatenate(sums[s], axis=1)
            high = total.astype(jnp.bfloat16)
            low = (total - high.astype(jnp.float32)).astype(jnp.bfloat16)
            rows_of += [high, low]
        added = jnp.dot(jnp.concatenate(rows_of, axis=0), pick, preferred_element_type=jnp.float32)
        one = added[0:groups] + added[groups : 2 * groups]
        two = added[2 * groups : 3 * groups] + added[3 * groups : 4 * groups]
        parts[layer, d, :, :] = jnp.where(lane_g < half, one, two)
        return carry

    sum_copies = []
    third = DIRS // 3
    for b in range(3):
        lax.fori_loop(b * third, (b + 1) * third, slopes, 0)
        for k in range(n_layer - 1):
            block = parts.at[layer, pl.ds(b * third, third)]
            sum_copies.append(send(block, block, ss_sem.at[k, b], sr_sem.at[k, b], peers[k]))
    for copy in sum_copies:
        copy.wait_recv()
    whole = parts[0]
    for k in range(1, n_layer):
        whole = whole + parts[k]
    out[0] = whole[:, :, :half]
    out[1] = whole[:, :, half:]

    for copy in edge_copies + mid_copies + col_copies + sum_copies:
        copy.wait_send()


def on_device(sizes, layers, wind, offsets, weights, sub_index):
    rows, cols = sub_index.shape
    tiles = cols // LANES
    groups = rows // SUB
    wide = groups + 2 * FOOT // SUB
    smem = pl.BlockSpec(memory_space=pltpu.SMEM)
    hbm = pl.BlockSpec(memory_space=pl.ANY)
    return pl.pallas_call(
        functools.partial(kernel, sizes),
        out_shape=jax.ShapeDtypeStruct((2, DIRS, groups, cols // SUB), jnp.float32),
        in_specs=[smem, smem, hbm, hbm, hbm],
        out_specs=pl.BlockSpec(memory_space=pltpu.VMEM),
        scratch_shapes=[
            pltpu.VMEM((tiles + 2, rows + 2 * RIM, LANES), jnp.float32),
            pltpu.VMEM((tiles + 2, SUB, wide, LANES), jnp.float32),
            pltpu.VMEM(weights.shape, weights.dtype),
            pltpu.VMEM((DIRS, 2, tiles, rows, LANES), jnp.float32),
            pltpu.VMEM(sub_index.shape, sub_index.dtype),
            pltpu.VMEM((sizes[0], DIRS, groups, LANES), jnp.float32),
            pltpu.SemaphoreType.DMA((tiles + 2,)),
            pltpu.SemaphoreType.DMA((tiles, 2)),
            pltpu.SemaphoreType.DMA((tiles, 2)),
            pltpu.SemaphoreType.DMA((2, 3)),
            pltpu.SemaphoreType.DMA((2, 3)),
            pltpu.SemaphoreType.DMA((sizes[0] - 1, 3)),
            pltpu.SemaphoreType.DMA((sizes[0] - 1, 3)),
        ],
        compiler_params=pltpu.CompilerParams(
            collective_id=0, has_side_effects=True, vmem_limit_bytes=32 * 1024 * 1024
        ),
    )(wind, offsets, layers, weights, sub_index)


def solution(mesh):
    sizes = (mesh.shape["layer"], mesh.shape["tx"], mesh.shape["ty"])
    placed = (
        P("layer", "tx", "ty"),
        P("layer", None),
        P("layer", None, None),
        P(None, None, "tx", "ty"),
        P("tx", "ty"),
    )
    return jax.shard_map(
        functools.partial(on_device, sizes),
        mesh=mesh, in_specs=placed, out_specs=P(None, None, "tx", "ty"), check_vma=False,
    )
```

```python
import functools

import jax
import jax.numpy as jnp
from jax import lax
from jax.experimental import pallas as pl
from jax.experimental.pallas import tpu as pltpu
from jax.sharding import PartitionSpec as P

DIRS = 9
SUB = 8
HMAX = 2
FOOT = 64
LANES = 128
RIM = 72
MESH = pl.DeviceIdType.MESH


def kernel(
    sizes, wind, offsets, layers, weights, sub_index, out, field, shifted, wraw, wlive, sub, parts,
    local_sem, xs_sem, xr_sem, zs_sem, zr_sem, ss_sem, sr_sem,
):
    n_layer, n_tx, n_ty = sizes
    rows, cols = sub_index.shape
    tiles = cols // LANES
    groups = rows // SUB
    last = tiles + 1
    foot_rows = RIM if n_tx > 2 else rows - RIM
    layer = lax.axis_index("layer")
    tx = lax.axis_index("tx")
    ty = lax.axis_index("ty")
    up = {"tx": lax.rem(tx + n_tx - 1, n_tx)}
    down = {"tx": lax.rem(tx + 1, n_tx)}
    left = {"ty": lax.rem(ty + n_ty - 1, n_ty)}
    right = {"ty": lax.rem(ty + 1, n_ty)}
    peers = [{"layer": lax.rem(layer + k, n_layer)} for k in range(1, n_layer)]

    own = []
    for c in range(tiles):
        copy = pltpu.make_async_copy(
            layers.at[0, :, pl.ds(c * LANES, LANES)],
            field.at[c + 1, pl.ds(RIM, rows), :],
            local_sem.at[c],
        )
        copy.start()
        own.append(copy)
    sub_copy = pltpu.make_async_copy(sub_index, sub, local_sem.at[tiles])
    sub_copy.start()
    weight_copy = pltpu.make_async_copy(weights, wraw, local_sem.at[tiles + 1])
    weight_copy.start()

    barrier = pltpu.get_barrier_semaphore()
    greeted = [up, left, right] if n_tx == 2 else [up, down, left, right]
    for device in greeted + peers:
        pl.semaphore_signal(barrier, inc=1, device_id=device, device_id_type=MESH)
    pl.semaphore_wait(barrier, len(greeted) + len(peers))

    def send(src, dst, send_sem, recv_sem, device):
        copy = pltpu.make_async_remote_copy(
            src_ref=src, dst_ref=dst, send_sem=send_sem, recv_sem=recv_sem,
            device_id=device, device_id_type=MESH,
        )
        copy.start()
        return copy

    def send_rows(c):
        return [
            send(
                field.at[c, pl.ds(rows, RIM), :], field.at[c, pl.ds(0, RIM), :],
                xs_sem.at[c - 1, 0], xr_sem.at[c - 1, 0], down,
            ),
            send(
                field.at[c, pl.ds(RIM, foot_rows), :], field.at[c, pl.ds(RIM + rows, foot_rows), :],
                xs_sem.at[c - 1, 1], xr_sem.at[c - 1, 1], up,
            ),
        ]

    def send_cols(start, size, k):
        return [
            send(
                field.at[tiles, pl.ds(start, size), :], field.at[0, pl.ds(start, size), :],
                zs_sem.at[0, k], zr_sem.at[0, k], right,
            ),
            send(
                field.at[1, pl.ds(start, size), :], field.at[last, pl.ds(start, size), :],
                zs_sem.at[1, k], zr_sem.at[1, k], left,
            ),
        ]

    for copy in own:
        copy.wait()
    edge_copies = send_rows(1) + send_rows(tiles)
    col_copies = send_cols(RIM, rows, 0)
    mid_copies = []
    for c in range(2, tiles):
        mid_copies += send_rows(c)

    sub_copy.wait()
    weight_copy.wait()

    def prepare(d, carry):
        for c in range(tiles):
            for g in range(0, groups, 2):
                live = (sub[pl.ds(g * SUB, 2 * SUB), pl.ds(c * LANES, LANES)] >= 0).astype(jnp.float32)
                for s in range(2):
                    both = wraw[d, s, pl.ds(g * SUB, 2 * SUB), pl.ds(c * LANES, LANES)].astype(jnp.float32) * live
                    for h in range(2):
                        wlive[d, s, c, pl.ds(g + h, SUB, stride=groups), :] = both[h * SUB : (h + 1) * SUB]
        return carry

    lax.fori_loop(0, 4, prepare, 0)
    for copy in edge_copies:
        copy.wait_recv()
    col_copies += send_cols(0, RIM, 1) + send_cols(RIM + rows, foot_rows, 2)
    lax.fori_loop(4, DIRS, prepare, 0)

    for copy in mid_copies:
        copy.wait_recv()
    for copy in col_copies:
        copy.wait_recv()
    if n_tx == 2:
        for c in range(tiles + 2):
            field[c, pl.ds(RIM + rows + foot_rows, RIM - foot_rows), :] = field[c, pl.ds(0, RIM - foot_rows), :]

    wide = rows // SUB + 2 * FOOT // SUB
    qrow = lax.shift_right_arithmetic(wind[0, 0], 6)
    qcol = lax.shift_right_arithmetic(wind[0, 1], 6)
    frow = (wind[0, 0] - 64 * qrow).astype(jnp.float32) / 64.0
    fcol = (wind[0, 1] - 64 * qcol).astype(jnp.float32) / 64.0
    lead = HMAX + 1 - qcol
    lane = lax.broadcasted_iota(jnp.int32, (wide, LANES), 1)

    def shift_phase(p, carry):
        mixed = []
        for c in range(tiles + 2):
            here = field[c, pl.ds(RIM - FOOT + p - qrow, wide, stride=SUB), :]
            above = field[c, pl.ds(RIM - FOOT - 1 + p - qrow, wide, stride=SUB), :]
            mixed.append((1.0 - frow) * here + frow * above)
        first = [pltpu.roll(m, (LANES - lead) & (LANES - 1), 1) for m in mixed]
        second = [pltpu.roll(m, (LANES + 1 - lead) & (LANES - 1), 1) for m in mixed]
        for c in range(tiles + 2):
            after = min(c + 1, last)
            one = jnp.where(lane < LANES - lead, first[c], first[after])
            two = jnp.where(lane < LANES + 1 - lead, second[c], second[after])
            shifted[c, p, :, :] = (1.0 - fcol) * one + fcol * two
        return carry

    lax.fori_loop(0, SUB, shift_phase, 0)

    lane_g = lax.broadcasted_iota(jnp.int32, (groups, LANES), 1)
    half = cols // SUB
    pick_row = lax.broadcasted_iota(jnp.int32, (cols, LANES), 0)
    pick_col = lax.broadcasted_iota(jnp.int32, (cols, LANES), 1)
    pick = (lax.shift_right_logical(pick_row, 3) == (pick_col & (half - 1))).astype(jnp.bfloat16)

    def slopes(d, carry):
        top = offsets[0, 0, d] + FOOT
        begin = offsets[0, 1, d] + LANES - HMAX - 1
        base = lax.shift_right_arithmetic(begin, 7)
        skip = begin & (LANES - 1)
        turn = (LANES - skip) & (LANES - 1)
        sums = [[None] * tiles for _ in range(2)]
        for r in range(SUB):
            row = top + r
            phase = row & (SUB - 1)
            first = lax.shift_right_arithmetic(row, 3)
            turned = [
                pltpu.roll(shifted[base + c, phase, pl.ds(first, groups), :], turn, 1) for c in range(tiles + 1)
            ]
            for c in range(tiles):
                view = jnp.where(lane_g < LANES - skip, turned[c], turned[c + 1])
                for s in range(2):
                    term = wlive[d, s, c, pl.ds(r * groups, groups), :] * view
                    sums[s][c] = term if r == 0 else sums[s][c] + term
        rows_of = []
        for s in range(2):
            total = jnp.concatenate(sums[s], axis=1)
            high = total.astype(jnp.bfloat16)
            low = (total - high.astype(jnp.float32)).astype(jnp.bfloat16)
            rows_of += [high, low]
        added = jnp.dot(jnp.concatenate(rows_of, axis=0), pick, preferred_element_type=jnp.float32)
        one = added[0:groups] + added[groups : 2 * groups]
        two = added[2 * groups : 3 * groups] + added[3 * groups : 4 * groups]
        parts[layer, d, :, :] = jnp.where(lane_g < half, one, two)
        return carry

    sum_copies = []
    third = DIRS // 3
    for b in range(3):
        lax.fori_loop(b * third, (b + 1) * third, slopes, 0)
        for k in range(n_layer - 1):
            block = parts.at[layer, pl.ds(b * third, third)]
            sum_copies.append(send(block, block, ss_sem.at[k, b], sr_sem.at[k, b], peers[k]))
    for copy in sum_copies:
        copy.wait_recv()
    whole = parts[0]
    for k in range(1, n_layer):
        whole = whole + parts[k]
    out[0] = whole[:, :, :half]
    out[1] = whole[:, :, half:]

    for copy in edge_copies + mid_copies + col_copies + sum_copies:
        copy.wait_send()


def on_device(sizes, layers, wind, offsets, weights, sub_index):
    rows, cols = sub_index.shape
    tiles = cols // LANES
    groups = rows // SUB
    wide = groups + 2 * FOOT // SUB
    smem = pl.BlockSpec(memory_space=pltpu.SMEM)
    hbm = pl.BlockSpec(memory_space=pltpu.HBM)
    return pl.pallas_call(
        functools.partial(kernel, sizes),
        out_shape=jax.ShapeDtypeStruct((2, DIRS, groups, cols // SUB), jnp.float32),
        in_specs=[smem, smem, hbm, hbm, hbm],
        out_specs=pl.BlockSpec(memory_space=pltpu.VMEM),
        scratch_shapes=[
            pltpu.VMEM((tiles + 2, rows + 2 * RIM, LANES), jnp.float32),
            pltpu.VMEM((tiles + 2, SUB, wide, LANES), jnp.float32),
            pltpu.VMEM(weights.shape, weights.dtype),
            pltpu.VMEM((DIRS, 2, tiles, rows, LANES), jnp.float32),
            pltpu.VMEM(sub_index.shape, sub_index.dtype),
            pltpu.VMEM((sizes[0], DIRS, groups, LANES), jnp.float32),
            pltpu.SemaphoreType.DMA((tiles + 2,)),
            pltpu.SemaphoreType.DMA((tiles, 2)),
            pltpu.SemaphoreType.DMA((tiles, 2)),
            pltpu.SemaphoreType.DMA((2, 3)),
            pltpu.SemaphoreType.DMA((2, 3)),
            pltpu.SemaphoreType.DMA((sizes[0] - 1, 3)),
            pltpu.SemaphoreType.DMA((sizes[0] - 1, 3)),
        ],
        compiler_params=pltpu.CompilerParams(
            collective_id=0, has_side_effects=True, vmem_limit_bytes=60 * 1024 * 1024
        ),
    )(wind, jnp.swapaxes(offsets, 1, 2), layers, weights, sub_index)


def solution(mesh):
    sizes = (mesh.shape["layer"], mesh.shape["tx"], mesh.shape["ty"])
    placed = (
        P("layer", "tx", "ty"),
        P("layer", None),
        P("layer", None, None),
        P(None, None, "tx", "ty"),
        P("tx", "ty"),
    )
    return jax.shard_map(
        functools.partial(on_device, sizes),
        mesh=mesh, in_specs=placed, out_specs=P(None, None, "tx", "ty"), check_vma=False,
    )
```

```python
import functools

import jax
import jax.numpy as jnp
from jax import lax
from jax.experimental import pallas as pl
from jax.experimental.pallas import tpu as pltpu
from jax.sharding import PartitionSpec as P

DIRS = 9
SUB = 8
HMAX = 2
FOOT = 64
LANES = 128
RIM = 72
MESH = pl.DeviceIdType.MESH


def kernel(
    sizes, wind, offsets, layers, weights, sub_index, out, field, side, shifted, wraw, wlive, sub, parts,
    local_sem, xs_sem, xr_sem, zs_sem, zr_sem, ss_sem, sr_sem,
):
    n_layer, n_tx, n_ty = sizes
    rows, cols = sub_index.shape
    tiles = cols // LANES
    groups = rows // SUB
    last = tiles + 1
    foot_rows = RIM if n_tx > 2 else rows - RIM
    layer = lax.axis_index("layer")
    tx = lax.axis_index("tx")
    ty = lax.axis_index("ty")
    up = {"tx": lax.rem(tx + n_tx - 1, n_tx)}
    down = {"tx": lax.rem(tx + 1, n_tx)}
    left = {"ty": lax.rem(ty + n_ty - 1, n_ty)}
    right = {"ty": lax.rem(ty + 1, n_ty)}
    peers = [{"layer": lax.rem(layer + k, n_layer)} for k in range(1, n_layer)]

    order = [0, tiles - 1] + list(range(1, tiles - 1))
    own = {}
    for c in order:
        own[c] = pltpu.make_async_copy(
            layers.at[0, :, pl.ds(c * LANES, LANES)],
            field.at[c, pl.ds(RIM, rows), :],
            local_sem.at[c],
        )
        own[c].start()

    barrier = pltpu.get_barrier_semaphore()
    greeted = [up, left, right] if n_tx == 2 else [up, down, left, right]
    for device in greeted + peers:
        pl.semaphore_signal(barrier, inc=1, device_id=device, device_id_type=MESH)
    pl.semaphore_wait(barrier, len(greeted) + len(peers))

    def send(src, dst, send_sem, recv_sem, device):
        copy = pltpu.make_async_remote_copy(
            src_ref=src, dst_ref=dst, send_sem=send_sem, recv_sem=recv_sem,
            device_id=device, device_id_type=MESH,
        )
        copy.start()
        return copy

    def send_rows(c):
        return [
            send(
                field.at[c, pl.ds(rows, RIM), :], field.at[c, pl.ds(0, RIM), :],
                xs_sem.at[c, 0], xr_sem.at[c, 0], down,
            ),
            send(
                field.at[c, pl.ds(RIM, foot_rows), :], field.at[c, pl.ds(RIM + rows, foot_rows), :],
                xs_sem.at[c, 1], xr_sem.at[c, 1], up,
            ),
        ]

    def send_cols(start, size, k):
        return [
            send(
                field.at[tiles - 1, pl.ds(start, size), :], side.at[0, pl.ds(start, size), :],
                zs_sem.at[0, k], zr_sem.at[0, k], right,
            ),
            send(
                field.at[0, pl.ds(start, size), :], side.at[1, pl.ds(start, size), :],
                zs_sem.at[1, k], zr_sem.at[1, k], left,
            ),
        ]

    edge_copies, mid_copies = [], []
    for c in order[:2]:
        own[c].wait()
        edge_copies += send_rows(c)
    col_copies = send_cols(RIM, rows, 0)
    for c in order[2:]:
        own[c].wait()
        mid_copies += send_rows(c)

    sub_copy = pltpu.make_async_copy(sub_index, sub, local_sem.at[tiles])
    sub_copy.start()
    weight_copy = pltpu.make_async_copy(weights, wraw, local_sem.at[tiles + 1])
    weight_copy.start()
    sub_copy.wait()
    weight_copy.wait()

    def prepare(d, carry):
        for c in range(tiles):
            for g in range(0, groups, 2):
                live = (sub[pl.ds(g * SUB, 2 * SUB), pl.ds(c * LANES, LANES)] >= 0).astype(jnp.float32)
                for s in range(2):
                    both = wraw[d, s, pl.ds(g * SUB, 2 * SUB), pl.ds(c * LANES, LANES)].astype(jnp.float32) * live
                    for h in range(2):
                        wlive[d, s, c, pl.ds(g + h, SUB, stride=groups), :] = both[h * SUB : (h + 1) * SUB]
        return carry

    lax.fori_loop(0, 4, prepare, 0)
    for copy in edge_copies:
        copy.wait_recv()
    col_copies += send_cols(0, RIM, 1) + send_cols(RIM + rows, foot_rows, 2)
    lax.fori_loop(4, DIRS, prepare, 0)

    def fill_foot(ref, count):
        if n_tx == 2:
            for c in range(count):
                ref[c, pl.ds(RIM + rows + foot_rows, RIM - foot_rows), :] = ref[c, pl.ds(0, RIM - foot_rows), :]

    wide = rows // SUB + 2 * FOOT // SUB
    qrow = lax.shift_right_arithmetic(wind[0, 0], 6)
    qcol = lax.shift_right_arithmetic(wind[0, 1], 6)
    frow = (wind[0, 0] - 64 * qrow).astype(jnp.float32) / 64.0
    fcol = (wind[0, 1] - 64 * qcol).astype(jnp.float32) / 64.0
    lead = HMAX + 1 - qcol
    lane = lax.broadcasted_iota(jnp.int32, (wide, LANES), 1)

    def mixed_rows(c, p):
        ref, at = (side, 0) if c == 0 else (side, 1) if c == last else (field, c - 1)
        here = ref[at, pl.ds(RIM - FOOT + p - qrow, wide, stride=SUB), :]
        above = ref[at, pl.ds(RIM - FOOT - 1 + p - qrow, wide, stride=SUB), :]
        return (1.0 - frow) * here + frow * above

    def shift_tiles(pairs):
        def phase(p, carry):
            first, second = {}, {}
            for c in sorted({c for pair in pairs for c in pair}):
                m = mixed_rows(c, p)
                first[c] = pltpu.roll(m, (LANES - lead) & (LANES - 1), 1)
                second[c] = pltpu.roll(m, (LANES + 1 - lead) & (LANES - 1), 1)
            for c, after in pairs:
                one = jnp.where(lane < LANES - lead, first[c], first[after])
                two = jnp.where(lane < LANES + 1 - lead, second[c], second[after])
                shifted[c, p, :, :] = (1.0 - fcol) * one + fcol * two
            return carry

        lax.fori_loop(0, SUB, phase, 0)

    lane_g = lax.broadcasted_iota(jnp.int32, (groups, LANES), 1)
    half = cols // SUB
    pick_row = lax.broadcasted_iota(jnp.int32, (cols, LANES), 0)
    pick_col = lax.broadcasted_iota(jnp.int32, (cols, LANES), 1)
    pick = (lax.shift_right_logical(pick_row, 3) == (pick_col & (half - 1))).astype(jnp.bfloat16)

    def slopes(chosen, fresh, d, carry):
        picked = jnp.concatenate([pick[c * LANES : (c + 1) * LANES] for c in chosen], axis=0)
        top = offsets[0, 0, d] + FOOT
        begin = offsets[0, 1, d] + LANES - HMAX - 1
        base = lax.shift_right_arithmetic(begin, 7)
        skip = begin & (LANES - 1)
        turn = (LANES - skip) & (LANES - 1)
        needed = sorted(set(chosen) | {c + 1 for c in chosen})
        sums = [{}, {}]
        for r in range(SUB):
            row = top + r
            phase = row & (SUB - 1)
            first = lax.shift_right_arithmetic(row, 3)
            turned = {c: pltpu.roll(shifted[base + c, phase, pl.ds(first, groups), :], turn, 1) for c in needed}
            for c in chosen:
                view = jnp.where(lane_g < LANES - skip, turned[c], turned[c + 1])
                for s in range(2):
                    term = wlive[d, s, c, pl.ds(r * groups, groups), :] * view
                    sums[s][c] = term if r == 0 else sums[s][c] + term
        rows_of = []
        for s in range(2):
            total = jnp.concatenate([sums[s][c] for c in chosen], axis=1)
            high = total.astype(jnp.bfloat16)
            low = (total - high.astype(jnp.float32)).astype(jnp.bfloat16)
            rows_of += [high, low]
        added = jnp.dot(jnp.concatenate(rows_of, axis=0), picked, preferred_element_type=jnp.float32)
        one = added[0:groups] + added[groups : 2 * groups]
        two = added[2 * groups : 3 * groups] + added[3 * groups : 4 * groups]
        slope = jnp.where(lane_g < half, one, two)
        parts[layer, d, :, :] = slope if fresh else parts[layer, d, :, :] + slope
        return carry

    for copy in mid_copies:
        copy.wait_recv()
    fill_foot(field, tiles)
    shift_tiles([(c, min(c + 1, tiles)) for c in range(1, tiles + 1)])
    lax.fori_loop(0, DIRS, functools.partial(slopes, list(range(1, tiles - 1)), True), 0)

    for copy in col_copies:
        copy.wait_recv()
    fill_foot(side, 2)
    shift_tiles([(0, 1), (tiles, last), (last, last)])

    sum_copies = []
    third = DIRS // 3
    for b in range(3):
        lax.fori_loop(b * third, (b + 1) * third, functools.partial(slopes, [0, tiles - 1], False), 0)
        for k in range(n_layer - 1):
            block = parts.at[layer, pl.ds(b * third, third)]
            sum_copies.append(send(block, block, ss_sem.at[k, b], sr_sem.at[k, b], peers[k]))
    for copy in sum_copies:
        copy.wait_recv()
    whole = parts[0]
    for k in range(1, n_layer):
        whole = whole + parts[k]
    out[0] = whole[:, :, :half]
    out[1] = whole[:, :, half:]

    for copy in edge_copies + mid_copies + col_copies + sum_copies:
        copy.wait_send()


def on_device(sizes, layers, wind, offsets, weights, sub_index):
    rows, cols = sub_index.shape
    tiles = cols // LANES
    groups = rows // SUB
    wide = groups + 2 * FOOT // SUB
    smem = pl.BlockSpec(memory_space=pltpu.SMEM)
    hbm = pl.BlockSpec(memory_space=pltpu.HBM)
    return pl.pallas_call(
        functools.partial(kernel, sizes),
        out_shape=jax.ShapeDtypeStruct((2, DIRS, groups, cols // SUB), jnp.float32),
        in_specs=[smem, smem, hbm, hbm, hbm],
        out_specs=pl.BlockSpec(memory_space=pltpu.VMEM),
        scratch_shapes=[
            pltpu.VMEM((tiles, rows + 2 * RIM, LANES), jnp.float32),
            pltpu.VMEM((2, rows + 2 * RIM, LANES), jnp.float32),
            pltpu.VMEM((tiles + 2, SUB, wide, LANES), jnp.float32),
            pltpu.VMEM(weights.shape, weights.dtype),
            pltpu.VMEM((DIRS, 2, tiles, rows, LANES), jnp.float32),
            pltpu.VMEM(sub_index.shape, sub_index.dtype),
            pltpu.VMEM((sizes[0], DIRS, groups, LANES), jnp.float32),
            pltpu.SemaphoreType.DMA((tiles + 2,)),
            pltpu.SemaphoreType.DMA((tiles, 2)),
            pltpu.SemaphoreType.DMA((tiles, 2)),
            pltpu.SemaphoreType.DMA((2, 3)),
            pltpu.SemaphoreType.DMA((2, 3)),
            pltpu.SemaphoreType.DMA((sizes[0] - 1, 3)),
            pltpu.SemaphoreType.DMA((sizes[0] - 1, 3)),
        ],
        compiler_params=pltpu.CompilerParams(
            collective_id=0, has_side_effects=True, vmem_limit_bytes=60 * 1024 * 1024
        ),
    )(wind, jnp.swapaxes(offsets, 1, 2), layers, weights, sub_index)


def solution(mesh):
    sizes = (mesh.shape["layer"], mesh.shape["tx"], mesh.shape["ty"])
    placed = (
        P("layer", "tx", "ty"),
        P("layer", None),
        P("layer", None, None),
        P(None, None, "tx", "ty"),
        P("tx", "ty"),
    )
    return jax.shard_map(
        functools.partial(on_device, sizes),
        mesh=mesh, in_specs=placed, out_specs=P(None, None, "tx", "ty"), check_vma=False,
    )
```

```python
import functools

import jax
import jax.numpy as jnp
from jax import lax
from jax.experimental import pallas as pl
from jax.experimental.pallas import tpu as pltpu
from jax.sharding import PartitionSpec as P

DIRS = 9
SUB = 8
HMAX = 2
FOOT = 64
LANES = 128
RIM = 72
MESH = pl.DeviceIdType.MESH


def kernel(
    sizes, wind, offsets, layers, weights, sub_index, out, field, side, shifted, wraw, wlive, sub, parts,
    local_sem, xs_sem, xr_sem, zs_sem, zr_sem, ss_sem, sr_sem,
):
    n_layer, n_tx, n_ty = sizes
    rows, cols = sub_index.shape
    tiles = cols // LANES
    groups = rows // SUB
    last = tiles + 1
    foot_rows = RIM if n_tx > 2 else rows - RIM
    layer = lax.axis_index("layer")
    tx = lax.axis_index("tx")
    ty = lax.axis_index("ty")
    up = {"tx": lax.rem(tx + n_tx - 1, n_tx)}
    down = {"tx": lax.rem(tx + 1, n_tx)}
    left = {"ty": lax.rem(ty + n_ty - 1, n_ty)}
    right = {"ty": lax.rem(ty + 1, n_ty)}
    peers = [{"layer": lax.rem(layer + k, n_layer)} for k in range(1, n_layer)]

    order = [0, tiles - 1] + list(range(1, tiles - 1))
    own = {}
    for c in order:
        own[c] = pltpu.make_async_copy(
            layers.at[0, :, pl.ds(c * LANES, LANES)],
            field.at[c, pl.ds(RIM, rows), :],
            local_sem.at[c],
        )
        own[c].start()

    sub_copy = pltpu.make_async_copy(sub_index, sub, local_sem.at[tiles])
    sub_copy.start()
    weight_copy = pltpu.make_async_copy(weights, wraw, local_sem.at[tiles + 1])
    weight_copy.start()

    barrier = pltpu.get_barrier_semaphore()
    greeted = [up, left, right] if n_tx == 2 else [up, down, left, right]
    for device in greeted + peers:
        pl.semaphore_signal(barrier, inc=1, device_id=device, device_id_type=MESH)
    pl.semaphore_wait(barrier, len(greeted) + len(peers))

    def send(src, dst, send_sem, recv_sem, device):
        copy = pltpu.make_async_remote_copy(
            src_ref=src, dst_ref=dst, send_sem=send_sem, recv_sem=recv_sem,
            device_id=device, device_id_type=MESH,
        )
        copy.start()
        return copy

    def send_rows(c):
        return [
            send(
                field.at[c, pl.ds(rows, RIM), :], field.at[c, pl.ds(0, RIM), :],
                xs_sem.at[c, 0], xr_sem.at[c, 0], down,
            ),
            send(
                field.at[c, pl.ds(RIM, foot_rows), :], field.at[c, pl.ds(RIM + rows, foot_rows), :],
                xs_sem.at[c, 1], xr_sem.at[c, 1], up,
            ),
        ]

    def send_cols(start, size, k):
        return [
            send(
                field.at[tiles - 1, pl.ds(start, size), :], side.at[0, pl.ds(start, size), :],
                zs_sem.at[0, k], zr_sem.at[0, k], right,
            ),
            send(
                field.at[0, pl.ds(start, size), :], side.at[1, pl.ds(start, size), :],
                zs_sem.at[1, k], zr_sem.at[1, k], left,
            ),
        ]

    edge_copies, mid_copies = [], []
    for c in order[:2]:
        own[c].wait()
        edge_copies += send_rows(c)
    col_copies = send_cols(RIM, rows, 0)
    for c in order[2:]:
        own[c].wait()
        mid_copies += send_rows(c)

    sub_copy.wait()
    weight_copy.wait()

    def prepare(d, carry):
        for c in range(tiles):
            for g in range(0, groups, 2):
                live = (sub[pl.ds(g * SUB, 2 * SUB), pl.ds(c * LANES, LANES)] >= 0).astype(jnp.float32)
                for s in range(2):
                    both = wraw[d, s, pl.ds(g * SUB, 2 * SUB), pl.ds(c * LANES, LANES)].astype(jnp.float32) * live
                    for h in range(2):
                        wlive[d, s, c, pl.ds(g + h, SUB, stride=groups), :] = both[h * SUB : (h + 1) * SUB]
        return carry

    lax.fori_loop(0, 4, prepare, 0)
    for copy in edge_copies:
        copy.wait_recv()
    col_copies += send_cols(0, RIM, 1) + send_cols(RIM + rows, foot_rows, 2)
    lax.fori_loop(4, DIRS, prepare, 0)

    def fill_foot(ref, count):
        if n_tx == 2:
            for c in range(count):
                ref[c, pl.ds(RIM + rows + foot_rows, RIM - foot_rows), :] = ref[c, pl.ds(0, RIM - foot_rows), :]

    wide = rows // SUB + 2 * FOOT // SUB
    qrow = lax.shift_right_arithmetic(wind[0, 0], 6)
    qcol = lax.shift_right_arithmetic(wind[0, 1], 6)
    frow = (wind[0, 0] - 64 * qrow).astype(jnp.float32) / 64.0
    fcol = (wind[0, 1] - 64 * qcol).astype(jnp.float32) / 64.0
    lead = HMAX + 1 - qcol
    lane = lax.broadcasted_iota(jnp.int32, (wide, LANES), 1)

    def mixed_rows(c, p):
        ref, at = (side, 0) if c == 0 else (side, 1) if c == last else (field, c - 1)
        here = ref[at, pl.ds(RIM - FOOT + p - qrow, wide, stride=SUB), :]
        above = ref[at, pl.ds(RIM - FOOT - 1 + p - qrow, wide, stride=SUB), :]
        return (1.0 - frow) * here + frow * above

    def shift_tiles(pairs):
        def phase(p, carry):
            first, second = {}, {}
            for c in sorted({c for pair in pairs for c in pair}):
                m = mixed_rows(c, p)
                first[c] = pltpu.roll(m, (LANES - lead) & (LANES - 1), 1)
                second[c] = pltpu.roll(m, (LANES + 1 - lead) & (LANES - 1), 1)
            for c, after in pairs:
                one = jnp.where(lane < LANES - lead, first[c], first[after])
                two = jnp.where(lane < LANES + 1 - lead, second[c], second[after])
                shifted[c, p, :, :] = (1.0 - fcol) * one + fcol * two
            return carry

        lax.fori_loop(0, SUB, phase, 0)

    lane_g = lax.broadcasted_iota(jnp.int32, (groups, LANES), 1)
    half = cols // SUB
    pick_row = lax.broadcasted_iota(jnp.int32, (cols, LANES), 0)
    pick_col = lax.broadcasted_iota(jnp.int32, (cols, LANES), 1)
    pick = (lax.shift_right_logical(pick_row, 3) == (pick_col & (half - 1))).astype(jnp.bfloat16)

    def slopes(chosen, fresh, d, carry):
        picked = jnp.concatenate([pick[c * LANES : (c + 1) * LANES] for c in chosen], axis=0)
        top = offsets[0, 0, d] + FOOT
        begin = offsets[0, 1, d] + LANES - HMAX - 1
        base = lax.shift_right_arithmetic(begin, 7)
        skip = begin & (LANES - 1)
        turn = (LANES - skip) & (LANES - 1)
        needed = sorted(set(chosen) | {c + 1 for c in chosen})
        sums = [{}, {}]
        for r in range(SUB):
            row = top + r
            phase = row & (SUB - 1)
            first = lax.shift_right_arithmetic(row, 3)
            turned = {c: pltpu.roll(shifted[base + c, phase, pl.ds(first, groups), :], turn, 1) for c in needed}
            for c in chosen:
                view = jnp.where(lane_g < LANES - skip, turned[c], turned[c + 1])
                for s in range(2):
                    term = wlive[d, s, c, pl.ds(r * groups, groups), :] * view
                    sums[s][c] = term if r == 0 else sums[s][c] + term
        rows_of = []
        for s in range(2):
            total = jnp.concatenate([sums[s][c] for c in chosen], axis=1)
            high = total.astype(jnp.bfloat16)
            low = (total - high.astype(jnp.float32)).astype(jnp.bfloat16)
            rows_of += [high, low]
        added = jnp.dot(jnp.concatenate(rows_of, axis=0), picked, preferred_element_type=jnp.float32)
        one = added[0:groups] + added[groups : 2 * groups]
        two = added[2 * groups : 3 * groups] + added[3 * groups : 4 * groups]
        slope = jnp.where(lane_g < half, one, two)
        parts[layer, d, :, :] = slope if fresh else parts[layer, d, :, :] + slope
        return carry

    for copy in mid_copies:
        copy.wait_recv()
    fill_foot(field, tiles)
    shift_tiles([(c, min(c + 1, tiles)) for c in range(1, tiles + 1)])
    lax.fori_loop(0, DIRS, functools.partial(slopes, list(range(1, tiles - 1)), True), 0)

    for copy in col_copies:
        copy.wait_recv()
    fill_foot(side, 2)
    shift_tiles([(0, 1), (tiles, last), (last, last)])

    sum_copies = []
    third = DIRS // 3
    for b in range(3):
        lax.fori_loop(b * third, (b + 1) * third, functools.partial(slopes, [0, tiles - 1], False), 0)
        for k in range(n_layer - 1):
            block = parts.at[layer, pl.ds(b * third, third)]
            sum_copies.append(send(block, block, ss_sem.at[k, b], sr_sem.at[k, b], peers[k]))
    for copy in sum_copies:
        copy.wait_recv()
    whole = parts[0]
    for k in range(1, n_layer):
        whole = whole + parts[k]
    out[0] = whole[:, :, :half]
    out[1] = whole[:, :, half:]

    for copy in edge_copies + mid_copies + col_copies + sum_copies:
        copy.wait_send()


def on_device(sizes, layers, wind, offsets, weights, sub_index):
    rows, cols = sub_index.shape
    tiles = cols // LANES
    groups = rows // SUB
    wide = groups + 2 * FOOT // SUB
    smem = pl.BlockSpec(memory_space=pltpu.SMEM)
    hbm = pl.BlockSpec(memory_space=pltpu.HBM)
    return pl.pallas_call(
        functools.partial(kernel, sizes),
        out_shape=jax.ShapeDtypeStruct((2, DIRS, groups, cols // SUB), jnp.float32),
        in_specs=[smem, smem, hbm, hbm, hbm],
        out_specs=pl.BlockSpec(memory_space=pltpu.VMEM),
        scratch_shapes=[
            pltpu.VMEM((tiles, rows + 2 * RIM, LANES), jnp.float32),
            pltpu.VMEM((2, rows + 2 * RIM, LANES), jnp.float32),
            pltpu.VMEM((tiles + 2, SUB, wide, LANES), jnp.float32),
            pltpu.VMEM(weights.shape, weights.dtype),
            pltpu.VMEM((DIRS, 2, tiles, rows, LANES), jnp.float32),
            pltpu.VMEM(sub_index.shape, sub_index.dtype),
            pltpu.VMEM((sizes[0], DIRS, groups, LANES), jnp.float32),
            pltpu.SemaphoreType.DMA((tiles + 2,)),
            pltpu.SemaphoreType.DMA((tiles, 2)),
            pltpu.SemaphoreType.DMA((tiles, 2)),
            pltpu.SemaphoreType.DMA((2, 3)),
            pltpu.SemaphoreType.DMA((2, 3)),
            pltpu.SemaphoreType.DMA((sizes[0] - 1, 3)),
            pltpu.SemaphoreType.DMA((sizes[0] - 1, 3)),
        ],
        compiler_params=pltpu.CompilerParams(
            collective_id=0, has_side_effects=True, vmem_limit_bytes=60 * 1024 * 1024
        ),
    )(wind, jnp.swapaxes(offsets, 1, 2), layers, weights, sub_index)


def solution(mesh):
    sizes = (mesh.shape["layer"], mesh.shape["tx"], mesh.shape["ty"])
    placed = (
        P("layer", "tx", "ty"),
        P("layer", None),
        P("layer", None, None),
        P(None, None, "tx", "ty"),
        P("tx", "ty"),
    )
    return jax.shard_map(
        functools.partial(on_device, sizes),
        mesh=mesh, in_specs=placed, out_specs=P(None, None, "tx", "ty"), check_vma=False,
    )
```

```python
import functools

import jax
import jax.numpy as jnp
from jax import lax
from jax.experimental import pallas as pl
from jax.experimental.pallas import tpu as pltpu
from jax.sharding import PartitionSpec as P

DIRS = 9
SUB = 8
HMAX = 2
FOOT = 64
LANES = 128
RIM = 72
MESH = pl.DeviceIdType.MESH


def kernel(
    sizes, wind, offsets, layers, weights, sub_index, out, field, shifted, wraw, wlive, sub, parts,
    local_sem, xs_sem, xr_sem, zs_sem, zr_sem, ss_sem, sr_sem,
):
    n_layer, n_tx, n_ty = sizes
    rows, cols = sub_index.shape
    tiles = cols // LANES
    groups = rows // SUB
    last = tiles + 1
    foot_rows = RIM if n_tx > 2 else rows - RIM
    layer = lax.axis_index("layer")
    tx = lax.axis_index("tx")
    ty = lax.axis_index("ty")
    up = {"tx": lax.rem(tx + n_tx - 1, n_tx)}
    down = {"tx": lax.rem(tx + 1, n_tx)}
    left = {"ty": lax.rem(ty + n_ty - 1, n_ty)}
    right = {"ty": lax.rem(ty + 1, n_ty)}
    peers = [{"layer": lax.rem(layer + k, n_layer)} for k in range(1, n_layer)]

    order = [0, tiles - 1] + list(range(1, tiles - 1))
    own = {}
    for c in order:
        copy = pltpu.make_async_copy(
            layers.at[0, :, pl.ds(c * LANES, LANES)],
            field.at[c + 1, pl.ds(RIM, rows), :],
            local_sem.at[c],
        )
        copy.start()
        own[c] = copy
    sub_copy = pltpu.make_async_copy(sub_index, sub, local_sem.at[tiles])
    sub_copy.start()
    weight_copy = pltpu.make_async_copy(weights, wraw, local_sem.at[tiles + 1])
    weight_copy.start()

    barrier = pltpu.get_barrier_semaphore()
    greeted = [up, left, right] if n_tx == 2 else [up, down, left, right]
    for device in greeted + peers:
        pl.semaphore_signal(barrier, inc=1, device_id=device, device_id_type=MESH)
    pl.semaphore_wait(barrier, len(greeted) + len(peers))

    def send(src, dst, send_sem, recv_sem, device):
        copy = pltpu.make_async_remote_copy(
            src_ref=src, dst_ref=dst, send_sem=send_sem, recv_sem=recv_sem,
            device_id=device, device_id_type=MESH,
        )
        copy.start()
        return copy

    def send_rows(c):
        return [
            send(
                field.at[c, pl.ds(rows, RIM), :], field.at[c, pl.ds(0, RIM), :],
                xs_sem.at[c - 1, 0], xr_sem.at[c - 1, 0], down,
            ),
            send(
                field.at[c, pl.ds(RIM, foot_rows), :], field.at[c, pl.ds(RIM + rows, foot_rows), :],
                xs_sem.at[c - 1, 1], xr_sem.at[c - 1, 1], up,
            ),
        ]

    def send_cols(start, size, k):
        return [
            send(
                field.at[tiles, pl.ds(start, size), :], field.at[0, pl.ds(start, size), :],
                zs_sem.at[0, k], zr_sem.at[0, k], right,
            ),
            send(
                field.at[1, pl.ds(start, size), :], field.at[last, pl.ds(start, size), :],
                zs_sem.at[1, k], zr_sem.at[1, k], left,
            ),
        ]

    edge_copies, mid_copies = [], []
    for c in order[:2]:
        own[c].wait()
        edge_copies += send_rows(c + 1)
    col_copies = send_cols(RIM, rows, 0)
    for c in order[2:]:
        own[c].wait()
        mid_copies += send_rows(c + 1)

    sub_copy.wait()
    weight_copy.wait()

    def prepare(d, carry):
        for c in range(tiles):
            for g in range(0, groups, 2):
                live = (sub[pl.ds(g * SUB, 2 * SUB), pl.ds(c * LANES, LANES)] >= 0).astype(jnp.float32)
                for s in range(2):
                    both = wraw[d, s, pl.ds(g * SUB, 2 * SUB), pl.ds(c * LANES, LANES)].astype(jnp.float32) * live
                    for h in range(2):
                        wlive[d, s, c, pl.ds(g + h, SUB, stride=groups), :] = both[h * SUB : (h + 1) * SUB]
        return carry

    lax.fori_loop(0, 4, prepare, 0)
    for copy in edge_copies:
        copy.wait_recv()
    col_copies += send_cols(0, RIM, 1) + send_cols(RIM + rows, foot_rows, 2)
    lax.fori_loop(4, DIRS, prepare, 0)

    for copy in mid_copies:
        copy.wait_recv()
    for copy in col_copies:
        copy.wait_recv()
    if n_tx == 2:
        for c in range(tiles + 2):
            field[c, pl.ds(RIM + rows + foot_rows, RIM - foot_rows), :] = field[c, pl.ds(0, RIM - foot_rows), :]

    wide = rows // SUB + 2 * FOOT // SUB
    qrow = lax.shift_right_arithmetic(wind[0, 0], 6)
    qcol = lax.shift_right_arithmetic(wind[0, 1], 6)
    frow = (wind[0, 0] - 64 * qrow).astype(jnp.float32) / 64.0
    fcol = (wind[0, 1] - 64 * qcol).astype(jnp.float32) / 64.0
    lead = HMAX + 1 - qcol
    lane = lax.broadcasted_iota(jnp.int32, (wide, LANES), 1)

    def shift_phase(p, carry):
        mixed = []
        for c in range(tiles + 2):
            here = field[c, pl.ds(RIM - FOOT + p - qrow, wide, stride=SUB), :]
            above = field[c, pl.ds(RIM - FOOT - 1 + p - qrow, wide, stride=SUB), :]
            mixed.append((1.0 - frow) * here + frow * above)
        first = [pltpu.roll(m, (LANES - lead) & (LANES - 1), 1) for m in mixed]
        second = [pltpu.roll(m, (LANES + 1 - lead) & (LANES - 1), 1) for m in mixed]
        for c in range(tiles + 2):
            after = min(c + 1, last)
            one = jnp.where(lane < LANES - lead, first[c], first[after])
            two = jnp.where(lane < LANES + 1 - lead, second[c], second[after])
            shifted[c, p, :, :] = (1.0 - fcol) * one + fcol * two
        return carry

    lax.fori_loop(0, SUB, shift_phase, 0)

    lane_g = lax.broadcasted_iota(jnp.int32, (groups, LANES), 1)
    half = cols // SUB
    pick_row = lax.broadcasted_iota(jnp.int32, (cols, LANES), 0)
    pick_col = lax.broadcasted_iota(jnp.int32, (cols, LANES), 1)
    pick = (lax.shift_right_logical(pick_row, 3) == (pick_col & (half - 1))).astype(jnp.bfloat16)

    def slopes(d, carry):
        top = offsets[0, 0, d] + FOOT
        begin = offsets[0, 1, d] + LANES - HMAX - 1
        base = lax.shift_right_arithmetic(begin, 7)
        skip = begin & (LANES - 1)
        turn = (LANES - skip) & (LANES - 1)
        sums = [[None] * tiles for _ in range(2)]
        for r in range(SUB):
            row = top + r
            phase = row & (SUB - 1)
            first = lax.shift_right_arithmetic(row, 3)
            turned = [
                pltpu.roll(shifted[base + c, phase, pl.ds(first, groups), :], turn, 1) for c in range(tiles + 1)
            ]
            for c in range(tiles):
                view = jnp.where(lane_g < LANES - skip, turned[c], turned[c + 1])
                for s in range(2):
                    term = wlive[d, s, c, pl.ds(r * groups, groups), :] * view
                    sums[s][c] = term if r == 0 else sums[s][c] + term
        rows_of = []
        for s in range(2):
            total = jnp.concatenate(sums[s], axis=1)
            high = total.astype(jnp.bfloat16)
            low = (total - high.astype(jnp.float32)).astype(jnp.bfloat16)
            rows_of += [high, low]
        added = jnp.dot(jnp.concatenate(rows_of, axis=0), pick, preferred_element_type=jnp.float32)
        one = added[0:groups] + added[groups : 2 * groups]
        two = added[2 * groups : 3 * groups] + added[3 * groups : 4 * groups]
        parts[layer, d, :, :] = jnp.where(lane_g < half, one, two)
        return carry

    sum_copies = []
    cuts = [0, 4, 7, DIRS]
    for b in range(3):
        lax.fori_loop(cuts[b], cuts[b + 1], slopes, 0)
        for k in range(n_layer - 1):
            block = parts.at[layer, pl.ds(cuts[b], cuts[b + 1] - cuts[b])]
            sum_copies.append(send(block, block, ss_sem.at[k, b], sr_sem.at[k, b], peers[k]))
    for copy in sum_copies:
        copy.wait_recv()
    whole = parts[0]
    for k in range(1, n_layer):
        whole = whole + parts[k]
    out[0] = whole[:, :, :half]
    out[1] = whole[:, :, half:]

    for copy in edge_copies + mid_copies + col_copies + sum_copies:
        copy.wait_send()


def on_device(sizes, layers, wind, offsets, weights, sub_index):
    rows, cols = sub_index.shape
    tiles = cols // LANES
    groups = rows // SUB
    wide = groups + 2 * FOOT // SUB
    smem = pl.BlockSpec(memory_space=pltpu.SMEM)
    hbm = pl.BlockSpec(memory_space=pltpu.HBM)
    return pl.pallas_call(
        functools.partial(kernel, sizes),
        out_shape=jax.ShapeDtypeStruct((2, DIRS, groups, cols // SUB), jnp.float32),
        in_specs=[smem, smem, hbm, hbm, hbm],
        out_specs=pl.BlockSpec(memory_space=pltpu.VMEM),
        scratch_shapes=[
            pltpu.VMEM((tiles + 2, rows + 2 * RIM, LANES), jnp.float32),
            pltpu.VMEM((tiles + 2, SUB, wide, LANES), jnp.float32),
            pltpu.VMEM(weights.shape, weights.dtype),
            pltpu.VMEM((DIRS, 2, tiles, rows, LANES), jnp.float32),
            pltpu.VMEM(sub_index.shape, sub_index.dtype),
            pltpu.VMEM((sizes[0], DIRS, groups, LANES), jnp.float32),
            pltpu.SemaphoreType.DMA((tiles + 2,)),
            pltpu.SemaphoreType.DMA((tiles, 2)),
            pltpu.SemaphoreType.DMA((tiles, 2)),
            pltpu.SemaphoreType.DMA((2, 3)),
            pltpu.SemaphoreType.DMA((2, 3)),
            pltpu.SemaphoreType.DMA((sizes[0] - 1, 3)),
            pltpu.SemaphoreType.DMA((sizes[0] - 1, 3)),
        ],
        compiler_params=pltpu.CompilerParams(
            collective_id=0, has_side_effects=True, vmem_limit_bytes=60 * 1024 * 1024
        ),
    )(wind, jnp.swapaxes(offsets, 1, 2), layers, weights, sub_index)


def solution(mesh):
    sizes = (mesh.shape["layer"], mesh.shape["tx"], mesh.shape["ty"])
    placed = (
        P("layer", "tx", "ty"),
        P("layer", None),
        P("layer", None, None),
        P(None, None, "tx", "ty"),
        P("tx", "ty"),
    )
    return jax.shard_map(
        functools.partial(on_device, sizes),
        mesh=mesh, in_specs=placed, out_specs=P(None, None, "tx", "ty"), check_vma=False,
    )
```

```python
import functools

import jax
import jax.numpy as jnp
from jax import lax
from jax.experimental import pallas as pl
from jax.experimental.pallas import tpu as pltpu
from jax.sharding import PartitionSpec as P

DIRS = 9
SUB = 8
HMAX = 2
FOOT = 64
LANES = 128
CUTS = (0, 1, 3, 5, 7, DIRS)
RIM = 72
MESH = pl.DeviceIdType.MESH


def kernel(
    sizes, wind, offsets, layers, weights, sub_index, out, field, shifted, wraw, wlive, sub, parts,
    local_sem, xs_sem, xr_sem, zs_sem, zr_sem, ss_sem, sr_sem,
):
    n_layer, n_tx, n_ty = sizes
    rows, cols = sub_index.shape
    tiles = cols // LANES
    groups = rows // SUB
    last = tiles + 1
    foot_rows = RIM if n_tx > 2 else rows - RIM
    layer = lax.axis_index("layer")
    tx = lax.axis_index("tx")
    ty = lax.axis_index("ty")
    up = {"tx": lax.rem(tx + n_tx - 1, n_tx)}
    down = {"tx": lax.rem(tx + 1, n_tx)}
    left = {"ty": lax.rem(ty + n_ty - 1, n_ty)}
    right = {"ty": lax.rem(ty + 1, n_ty)}
    peers = [{"layer": lax.rem(layer + k, n_layer)} for k in range(1, n_layer)]

    order = [0, tiles - 1] + list(range(1, tiles - 1))
    own = {}
    for c in order:
        copy = pltpu.make_async_copy(
            layers.at[0, :, pl.ds(c * LANES, LANES)],
            field.at[c + 1, pl.ds(RIM, rows), :],
            local_sem.at[c],
        )
        copy.start()
        own[c] = copy
    sub_copy = pltpu.make_async_copy(sub_index, sub, local_sem.at[tiles])
    sub_copy.start()
    weight_copy = pltpu.make_async_copy(weights, wraw, local_sem.at[tiles + 1])
    weight_copy.start()

    barrier = pltpu.get_barrier_semaphore()
    greeted = [up, left, right] if n_tx == 2 else [up, down, left, right]
    for device in greeted + peers:
        pl.semaphore_signal(barrier, inc=1, device_id=device, device_id_type=MESH)
    pl.semaphore_wait(barrier, len(greeted) + len(peers))

    def send(src, dst, send_sem, recv_sem, device):
        copy = pltpu.make_async_remote_copy(
            src_ref=src, dst_ref=dst, send_sem=send_sem, recv_sem=recv_sem,
            device_id=device, device_id_type=MESH,
        )
        copy.start()
        return copy

    def send_rows(c):
        return [
            send(
                field.at[c, pl.ds(rows, RIM), :], field.at[c, pl.ds(0, RIM), :],
                xs_sem.at[c - 1, 0], xr_sem.at[c - 1, 0], down,
            ),
            send(
                field.at[c, pl.ds(RIM, foot_rows), :], field.at[c, pl.ds(RIM + rows, foot_rows), :],
                xs_sem.at[c - 1, 1], xr_sem.at[c - 1, 1], up,
            ),
        ]

    def send_cols(start, size, k):
        return [
            send(
                field.at[tiles, pl.ds(start, size), :], field.at[0, pl.ds(start, size), :],
                zs_sem.at[0, k], zr_sem.at[0, k], right,
            ),
            send(
                field.at[1, pl.ds(start, size), :], field.at[last, pl.ds(start, size), :],
                zs_sem.at[1, k], zr_sem.at[1, k], left,
            ),
        ]

    edge_copies, mid_copies = [], []
    for c in order[:2]:
        own[c].wait()
        edge_copies += send_rows(c + 1)
    col_copies = send_cols(RIM, rows, 0)
    for c in order[2:]:
        own[c].wait()
        mid_copies += send_rows(c + 1)

    sub_copy.wait()
    weight_copy.wait()

    def prepare(d, carry):
        for c in range(tiles):
            for g in range(0, groups, 2):
                live = (sub[pl.ds(g * SUB, 2 * SUB), pl.ds(c * LANES, LANES)] >= 0).astype(jnp.float32)
                for s in range(2):
                    both = wraw[d, s, pl.ds(g * SUB, 2 * SUB), pl.ds(c * LANES, LANES)].astype(jnp.float32) * live
                    for h in range(2):
                        wlive[d, s, c, pl.ds(g + h, SUB, stride=groups), :] = both[h * SUB : (h + 1) * SUB]
        return carry

    lax.fori_loop(0, 4, prepare, 0)
    for copy in edge_copies:
        copy.wait_recv()
    col_copies += send_cols(0, RIM, 1) + send_cols(RIM + rows, foot_rows, 2)
    lax.fori_loop(4, DIRS, prepare, 0)

    for copy in mid_copies:
        copy.wait_recv()
    for copy in col_copies:
        copy.wait_recv()
    if n_tx == 2:
        for c in range(tiles + 2):
            field[c, pl.ds(RIM + rows + foot_rows, RIM - foot_rows), :] = field[c, pl.ds(0, RIM - foot_rows), :]

    wide = rows // SUB + 2 * FOOT // SUB
    qrow = lax.shift_right_arithmetic(wind[0, 0], 6)
    qcol = lax.shift_right_arithmetic(wind[0, 1], 6)
    frow = (wind[0, 0] - 64 * qrow).astype(jnp.float32) / 64.0
    fcol = (wind[0, 1] - 64 * qcol).astype(jnp.float32) / 64.0
    lead = HMAX + 1 - qcol
    lane = lax.broadcasted_iota(jnp.int32, (wide, LANES), 1)

    def shift_phase(p, carry):
        mixed = []
        for c in range(tiles + 2):
            here = field[c, pl.ds(RIM - FOOT + p - qrow, wide, stride=SUB), :]
            above = field[c, pl.ds(RIM - FOOT - 1 + p - qrow, wide, stride=SUB), :]
            mixed.append((1.0 - frow) * here + frow * above)
        first = [pltpu.roll(m, (LANES - lead) & (LANES - 1), 1) for m in mixed]
        second = [pltpu.roll(m, (LANES + 1 - lead) & (LANES - 1), 1) for m in mixed]
        for c in range(tiles + 2):
            after = min(c + 1, last)
            one = jnp.where(lane < LANES - lead, first[c], first[after])
            two = jnp.where(lane < LANES + 1 - lead, second[c], second[after])
            shifted[c, p, :, :] = (1.0 - fcol) * one + fcol * two
        return carry

    lax.fori_loop(0, SUB, shift_phase, 0)

    lane_g = lax.broadcasted_iota(jnp.int32, (groups, LANES), 1)
    half = cols // SUB
    pick_row = lax.broadcasted_iota(jnp.int32, (cols, LANES), 0)
    pick_col = lax.broadcasted_iota(jnp.int32, (cols, LANES), 1)
    pick = (lax.shift_right_logical(pick_row, 3) == (pick_col & (half - 1))).astype(jnp.bfloat16)

    def slopes(d, carry):
        top = offsets[0, 0, d] + FOOT
        begin = offsets[0, 1, d] + LANES - HMAX - 1
        base = lax.shift_right_arithmetic(begin, 7)
        skip = begin & (LANES - 1)
        turn = (LANES - skip) & (LANES - 1)
        sums = [[None] * tiles for _ in range(2)]
        for r in range(SUB):
            row = top + r
            phase = row & (SUB - 1)
            first = lax.shift_right_arithmetic(row, 3)
            turned = [
                pltpu.roll(shifted[base + c, phase, pl.ds(first, groups), :], turn, 1) for c in range(tiles + 1)
            ]
            for c in range(tiles):
                view = jnp.where(lane_g < LANES - skip, turned[c], turned[c + 1])
                for s in range(2):
                    term = wlive[d, s, c, pl.ds(r * groups, groups), :] * view
                    sums[s][c] = term if r == 0 else sums[s][c] + term
        rows_of = []
        for s in range(2):
            total = jnp.concatenate(sums[s], axis=1)
            high = total.astype(jnp.bfloat16)
            low = (total - high.astype(jnp.float32)).astype(jnp.bfloat16)
            rows_of += [high, low]
        added = jnp.dot(jnp.concatenate(rows_of, axis=0), pick, preferred_element_type=jnp.float32)
        one = added[0:groups] + added[groups : 2 * groups]
        two = added[2 * groups : 3 * groups] + added[3 * groups : 4 * groups]
        parts[layer, d, :, :] = jnp.where(lane_g < half, one, two)
        return carry

    sum_copies = []
    cuts = CUTS
    for b in range(len(cuts) - 1):
        lax.fori_loop(cuts[b], cuts[b + 1], slopes, 0)
        for k in range(n_layer - 1):
            block = parts.at[layer, pl.ds(cuts[b], cuts[b + 1] - cuts[b])]
            sum_copies.append(send(block, block, ss_sem.at[k, b], sr_sem.at[k, b], peers[k]))
    for copy in sum_copies:
        copy.wait_recv()
    whole = parts[0]
    for k in range(1, n_layer):
        whole = whole + parts[k]
    out[0] = whole[:, :, :half]
    out[1] = whole[:, :, half:]

    for copy in edge_copies + mid_copies + col_copies + sum_copies:
        copy.wait_send()


def on_device(sizes, layers, wind, offsets, weights, sub_index):
    rows, cols = sub_index.shape
    tiles = cols // LANES
    groups = rows // SUB
    wide = groups + 2 * FOOT // SUB
    smem = pl.BlockSpec(memory_space=pltpu.SMEM)
    hbm = pl.BlockSpec(memory_space=pltpu.HBM)
    return pl.pallas_call(
        functools.partial(kernel, sizes),
        out_shape=jax.ShapeDtypeStruct((2, DIRS, groups, cols // SUB), jnp.float32),
        in_specs=[smem, smem, hbm, hbm, hbm],
        out_specs=pl.BlockSpec(memory_space=pltpu.VMEM),
        scratch_shapes=[
            pltpu.VMEM((tiles + 2, rows + 2 * RIM, LANES), jnp.float32),
            pltpu.VMEM((tiles + 2, SUB, wide, LANES), jnp.float32),
            pltpu.VMEM(weights.shape, weights.dtype),
            pltpu.VMEM((DIRS, 2, tiles, rows, LANES), jnp.float32),
            pltpu.VMEM(sub_index.shape, sub_index.dtype),
            pltpu.VMEM((sizes[0], DIRS, groups, LANES), jnp.float32),
            pltpu.SemaphoreType.DMA((tiles + 2,)),
            pltpu.SemaphoreType.DMA((tiles, 2)),
            pltpu.SemaphoreType.DMA((tiles, 2)),
            pltpu.SemaphoreType.DMA((2, 3)),
            pltpu.SemaphoreType.DMA((2, 3)),
            pltpu.SemaphoreType.DMA((sizes[0] - 1, len(CUTS) - 1)),
            pltpu.SemaphoreType.DMA((sizes[0] - 1, len(CUTS) - 1)),
        ],
        compiler_params=pltpu.CompilerParams(
            collective_id=0, has_side_effects=True, vmem_limit_bytes=60 * 1024 * 1024
        ),
    )(wind, jnp.swapaxes(offsets, 1, 2), layers, weights, sub_index)


def solution(mesh):
    sizes = (mesh.shape["layer"], mesh.shape["tx"], mesh.shape["ty"])
    placed = (
        P("layer", "tx", "ty"),
        P("layer", None),
        P("layer", None, None),
        P(None, None, "tx", "ty"),
        P("tx", "ty"),
    )
    return jax.shard_map(
        functools.partial(on_device, sizes),
        mesh=mesh, in_specs=placed, out_specs=P(None, None, "tx", "ty"), check_vma=False,
    )
```

```python
import functools

import jax
import jax.numpy as jnp
from jax import lax
from jax.experimental import pallas as pl
from jax.experimental.pallas import tpu as pltpu
from jax.sharding import PartitionSpec as P

DIRS = 9
SUB = 8
HMAX = 2
FOOT = 64
LANES = 128
CUTS = (0, 1, 3, 5, 7, DIRS)
RIM = 72
MESH = pl.DeviceIdType.MESH


def kernel(
    sizes, wind, offsets, layers, weights, sub_index, out, field, shifted, wraw, wlive, sub, parts,
    local_sem, xs_sem, xr_sem, zs_sem, zr_sem, ss_sem, sr_sem,
):
    n_layer, n_tx, n_ty = sizes
    rows, cols = sub_index.shape
    tiles = cols // LANES
    groups = rows // SUB
    last = tiles + 1
    foot_rows = RIM if n_tx > 2 else rows - RIM
    layer = lax.axis_index("layer")
    tx = lax.axis_index("tx")
    ty = lax.axis_index("ty")
    up = {"tx": lax.rem(tx + n_tx - 1, n_tx)}
    down = {"tx": lax.rem(tx + 1, n_tx)}
    left = {"ty": lax.rem(ty + n_ty - 1, n_ty)}
    right = {"ty": lax.rem(ty + 1, n_ty)}
    peers = [{"layer": lax.rem(layer + k, n_layer)} for k in range(1, n_layer)]

    order = [0, tiles - 1] + list(range(1, tiles - 1))
    own = {}
    for c in order:
        copy = pltpu.make_async_copy(
            layers.at[0, :, pl.ds(c * LANES, LANES)],
            field.at[c + 1, pl.ds(RIM, rows), :],
            local_sem.at[c],
        )
        copy.start()
        own[c] = copy
    sub_copy = pltpu.make_async_copy(sub_index, sub, local_sem.at[tiles])
    sub_copy.start()
    weight_copy = pltpu.make_async_copy(weights, wraw, local_sem.at[tiles + 1])
    weight_copy.start()

    barrier = pltpu.get_barrier_semaphore()
    greeted = [up, left, right] if n_tx == 2 else [up, down, left, right]
    for device in greeted + peers:
        pl.semaphore_signal(barrier, inc=1, device_id=device, device_id_type=MESH)
    pl.semaphore_wait(barrier, len(greeted) + len(peers))

    def send(src, dst, send_sem, recv_sem, device):
        copy = pltpu.make_async_remote_copy(
            src_ref=src, dst_ref=dst, send_sem=send_sem, recv_sem=recv_sem,
            device_id=device, device_id_type=MESH,
        )
        copy.start()
        return copy

    def send_rows(c):
        return [
            send(
                field.at[c, pl.ds(rows, RIM), :], field.at[c, pl.ds(0, RIM), :],
                xs_sem.at[c - 1, 0], xr_sem.at[c - 1, 0], down,
            ),
            send(
                field.at[c, pl.ds(RIM, foot_rows), :], field.at[c, pl.ds(RIM + rows, foot_rows), :],
                xs_sem.at[c - 1, 1], xr_sem.at[c - 1, 1], up,
            ),
        ]

    def send_cols(start, size, k):
        return [
            send(
                field.at[tiles, pl.ds(start, size), :], field.at[0, pl.ds(start, size), :],
                zs_sem.at[0, k], zr_sem.at[0, k], right,
            ),
            send(
                field.at[1, pl.ds(start, size), :], field.at[last, pl.ds(start, size), :],
                zs_sem.at[1, k], zr_sem.at[1, k], left,
            ),
        ]

    edge_copies, mid_copies = [], []
    for c in order[:2]:
        own[c].wait()
        edge_copies += send_rows(c + 1)
    for c in order[2:]:
        own[c].wait()
        mid_copies += send_rows(c + 1)
    col_copies = send_cols(RIM, rows, 0)

    sub_copy.wait()
    weight_copy.wait()

    def prepare(d, carry):
        for c in range(tiles):
            for g in range(0, groups, 2):
                live = (sub[pl.ds(g * SUB, 2 * SUB), pl.ds(c * LANES, LANES)] >= 0).astype(jnp.float32)
                for s in range(2):
                    both = wraw[d, s, pl.ds(g * SUB, 2 * SUB), pl.ds(c * LANES, LANES)].astype(jnp.float32) * live
                    for h in range(2):
                        wlive[d, s, c, pl.ds(g + h, SUB, stride=groups), :] = both[h * SUB : (h + 1) * SUB]
        return carry

    lax.fori_loop(0, 4, prepare, 0)
    for copy in edge_copies:
        copy.wait_recv()
    col_copies += send_cols(0, RIM, 1) + send_cols(RIM + rows, foot_rows, 2)
    lax.fori_loop(4, DIRS, prepare, 0)

    for copy in mid_copies:
        copy.wait_recv()
    for copy in col_copies:
        copy.wait_recv()
    if n_tx == 2:
        for c in range(tiles + 2):
            field[c, pl.ds(RIM + rows + foot_rows, RIM - foot_rows), :] = field[c, pl.ds(0, RIM - foot_rows), :]

    wide = rows // SUB + 2 * FOOT // SUB
    qrow = lax.shift_right_arithmetic(wind[0, 0], 6)
    qcol = lax.shift_right_arithmetic(wind[0, 1], 6)
    frow = (wind[0, 0] - 64 * qrow).astype(jnp.float32) / 64.0
    fcol = (wind[0, 1] - 64 * qcol).astype(jnp.float32) / 64.0
    lead = HMAX + 1 - qcol
    lane = lax.broadcasted_iota(jnp.int32, (wide, LANES), 1)

    def shift_phase(p, carry):
        mixed = []
        for c in range(tiles + 2):
            here = field[c, pl.ds(RIM - FOOT + p - qrow, wide, stride=SUB), :]
            above = field[c, pl.ds(RIM - FOOT - 1 + p - qrow, wide, stride=SUB), :]
            mixed.append((1.0 - frow) * here + frow * above)
        first = [pltpu.roll(m, (LANES - lead) & (LANES - 1), 1) for m in mixed]
        second = [pltpu.roll(m, (LANES + 1 - lead) & (LANES - 1), 1) for m in mixed]
        for c in range(tiles + 2):
            after = min(c + 1, last)
            one = jnp.where(lane < LANES - lead, first[c], first[after])
            two = jnp.where(lane < LANES + 1 - lead, second[c], second[after])
            shifted[c, p, :, :] = (1.0 - fcol) * one + fcol * two
        return carry

    lax.fori_loop(0, SUB, shift_phase, 0)

    lane_g = lax.broadcasted_iota(jnp.int32, (groups, LANES), 1)
    half = cols // SUB
    pick_row = lax.broadcasted_iota(jnp.int32, (cols, LANES), 0)
    pick_col = lax.broadcasted_iota(jnp.int32, (cols, LANES), 1)
    pick = (lax.shift_right_logical(pick_row, 3) == (pick_col & (half - 1))).astype(jnp.bfloat16)

    def slopes(d, carry):
        top = offsets[0, 0, d] + FOOT
        begin = offsets[0, 1, d] + LANES - HMAX - 1
        base = lax.shift_right_arithmetic(begin, 7)
        skip = begin & (LANES - 1)
        turn = (LANES - skip) & (LANES - 1)
        sums = [[None] * tiles for _ in range(2)]
        for r in range(SUB):
            row = top + r
            phase = row & (SUB - 1)
            first = lax.shift_right_arithmetic(row, 3)
            turned = [
                pltpu.roll(shifted[base + c, phase, pl.ds(first, groups), :], turn, 1) for c in range(tiles + 1)
            ]
            for c in range(tiles):
                view = jnp.where(lane_g < LANES - skip, turned[c], turned[c + 1])
                for s in range(2):
                    term = wlive[d, s, c, pl.ds(r * groups, groups), :] * view
                    sums[s][c] = term if r == 0 else sums[s][c] + term
        rows_of = []
        for s in range(2):
            total = jnp.concatenate(sums[s], axis=1)
            high = total.astype(jnp.bfloat16)
            low = (total - high.astype(jnp.float32)).astype(jnp.bfloat16)
            rows_of += [high, low]
        added = jnp.dot(jnp.concatenate(rows_of, axis=0), pick, preferred_element_type=jnp.float32)
        one = added[0:groups] + added[groups : 2 * groups]
        two = added[2 * groups : 3 * groups] + added[3 * groups : 4 * groups]
        parts[layer, d, :, :] = jnp.where(lane_g < half, one, two)
        return carry

    sum_copies = []
    cuts = CUTS
    for b in range(len(cuts) - 1):
        lax.fori_loop(cuts[b], cuts[b + 1], slopes, 0)
        for k in range(n_layer - 1):
            block = parts.at[layer, pl.ds(cuts[b], cuts[b + 1] - cuts[b])]
            sum_copies.append(send(block, block, ss_sem.at[k, b], sr_sem.at[k, b], peers[k]))
    for copy in sum_copies:
        copy.wait_recv()
    whole = parts[0]
    for k in range(1, n_layer):
        whole = whole + parts[k]
    out[0] = whole[:, :, :half]
    out[1] = whole[:, :, half:]

    for copy in edge_copies + mid_copies + col_copies + sum_copies:
        copy.wait_send()


def on_device(sizes, layers, wind, offsets, weights, sub_index):
    rows, cols = sub_index.shape
    tiles = cols // LANES
    groups = rows // SUB
    wide = groups + 2 * FOOT // SUB
    smem = pl.BlockSpec(memory_space=pltpu.SMEM)
    hbm = pl.BlockSpec(memory_space=pltpu.HBM)
    return pl.pallas_call(
        functools.partial(kernel, sizes),
        out_shape=jax.ShapeDtypeStruct((2, DIRS, groups, cols // SUB), jnp.float32),
        in_specs=[smem, smem, hbm, hbm, hbm],
        out_specs=pl.BlockSpec(memory_space=pltpu.VMEM),
        scratch_shapes=[
            pltpu.VMEM((tiles + 2, rows + 2 * RIM, LANES), jnp.float32),
            pltpu.VMEM((tiles + 2, SUB, wide, LANES), jnp.float32),
            pltpu.VMEM(weights.shape, weights.dtype),
            pltpu.VMEM((DIRS, 2, tiles, rows, LANES), jnp.float32),
            pltpu.VMEM(sub_index.shape, sub_index.dtype),
            pltpu.VMEM((sizes[0], DIRS, groups, LANES), jnp.float32),
            pltpu.SemaphoreType.DMA((tiles + 2,)),
            pltpu.SemaphoreType.DMA((tiles, 2)),
            pltpu.SemaphoreType.DMA((tiles, 2)),
            pltpu.SemaphoreType.DMA((2, 3)),
            pltpu.SemaphoreType.DMA((2, 3)),
            pltpu.SemaphoreType.DMA((sizes[0] - 1, len(CUTS) - 1)),
            pltpu.SemaphoreType.DMA((sizes[0] - 1, len(CUTS) - 1)),
        ],
        compiler_params=pltpu.CompilerParams(
            collective_id=0, has_side_effects=True, vmem_limit_bytes=60 * 1024 * 1024
        ),
    )(wind, jnp.swapaxes(offsets, 1, 2), layers, weights, sub_index)


def solution(mesh):
    sizes = (mesh.shape["layer"], mesh.shape["tx"], mesh.shape["ty"])
    placed = (
        P("layer", "tx", "ty"),
        P("layer", None),
        P("layer", None, None),
        P(None, None, "tx", "ty"),
        P("tx", "ty"),
    )
    return jax.shard_map(
        functools.partial(on_device, sizes),
        mesh=mesh, in_specs=placed, out_specs=P(None, None, "tx", "ty"), check_vma=False,
    )
```
